32 devices in a mesh: parts: 2 (over y), lat: 2 (over core), lon: 8 (over z, x).
Axes of the slice: x: 2, y: 2, z: 4, core: 2. Of those that a mesh axis runs over, the one named last changes fastest.
Arguments:
- fields: bfloat16 [256, 64, 512], P(('parts', 'lat'), 'lon'), parts along dimension 0, may hold values from -6 to 6
- psi_near: bfloat16 [128, 4, 3, 3], replicated, may hold values from -2 to 2
- psi_far: bfloat16 [4, 2, 4, 3, 16], replicated, may hold values from -0.625 to 0.625
- blocks: int32 [4, 2], replicated, may hold values from 0 to 3, all different within a row
- weight: bfloat16 [4, 512, 512], replicated, may hold values from -0.125 to 0.125
- out_bias: float32 [512], replicated, may hold values from -6 to 6
- cotangent: bfloat16 [256, 64, 512], P(('parts', 'lat'), 'lon'), parts along dimension 0, may hold values from -6 to 6
Outputs:
- layer_out: bfloat16 [256, 64, 512], P(('parts', 'lat'), 'lon'), parts along dimension 0
- grad_fields: bfloat16 [256, 64, 512], P(('parts', 'lat'), 'lon'), parts along dimension 0
- grad_weight: float32 [4, 1024, 512], P(None, ('parts', 'lat', 'lon')), parts along dimension 1
- grad_bias: float32 [1024], P(('parts', 'lat', 'lon')), parts along dimension 0
The draws below stay inside these ranges and needn't reach their ends.
There are 2 independent parts, one for each index of `parts`. The reference program is written for one: setup_inputs(seed, part) draws one part's arguments, and reference() takes and returns one part's arrays. A program takes and returns all parts, laid end to end along the dimension named above; an argument that names none is the same for every part. Nothing has to cross between parts.
Inputs may be any that keep to these rules, and one draw needn't show every extreme that they name: Each of the 4 polar rows names 2 different blocks; every block is named by some row.
All inputs are finite; a program needn't handle non-finite values.
Results may differ from the reference program's by a relative error of at most 0.005.
Values may be sent and summed in bfloat16 or wider, within the bound.
A program may use at most 128 MiB of HBM per device.

```python
import math
import jax
import jax.numpy as jnp
from jax import lax

C = 512
K = 4
BW = 16
P_SIZE = 4
NLAT = 128
NLON = 64
NBLK = 4
NB = 2


def shard_levels(rng, extent, shards, low, high):
    level = 1.0
    for dim, parts in shards:
        heights = jax.random.uniform(jax.random.fold_in(jax.random.fold_in(rng, 6), dim), (parts,), jnp.float32, low / len(shards), high / len(shards))
        level = level * jnp.repeat(jnp.exp(heights), extent[dim] // parts).reshape((-1,) + (1,) * (len(extent) - 1 - dim))
    return level


def choose_distinct(key, rows, count, top, lift):
    ranking = jax.random.permutation(jax.random.fold_in(key, 1), count)
    favour = ranking
    for power in range(3):
        favour = favour * favour // count
    favour = favour * lift // count
    tickets = jax.random.randint(jax.random.fold_in(key, 2), (rows, count), 0, 4096) + favour
    fixed_rows = jax.random.permutation(jax.random.fold_in(key, 3), rows)[jnp.arange(count) % rows]
    tickets = jnp.where(jnp.arange(rows)[:, None] == fixed_rows[None, :], 1 << 14, tickets)
    score = tickets * count + jnp.arange(count)
    return lax.top_k(score.astype(jnp.int32), top)[1].astype(jnp.int32)


def bell_draw(stream_key, extent, deviation, most, shards=(), kind=jnp.bfloat16):
    factor_of = shard_levels(stream_key, extent, shards, -0.22, 0.18) if shards else 1.0
    entries = jax.random.normal(stream_key, extent, jnp.float32) * deviation * factor_of
    return jnp.minimum(jnp.maximum(entries, -most), most).astype(kind)


def setup_inputs(seed: int = 0, part: int = 0) -> dict:
    keys = jax.random.split(jax.random.key(seed), 8)
    own_keys = jax.random.split(jax.random.fold_in(keys[7], part), 8)
    return {
        "fields": bell_draw(own_keys[0], (NLAT, NLON, C), 1.0, 6.0, ((0, 2), (1, 8))),
        "psi_near": bell_draw(keys[1], (NLAT, K, 3, 3), 9 ** -0.5, 2.0),
        "psi_far": bell_draw(keys[2], (P_SIZE, NB, K, 3, BW), (3 * NB * BW) ** -0.5, 0.625),
        "blocks": choose_distinct(keys[3], P_SIZE, NBLK, NB, 0),
        "weight": bell_draw(keys[4], (K, C, C), (K * C) ** -0.5, 0.125),
        "out_bias": bell_draw(keys[5], (C,), 1.0, 6.0, (), jnp.float32),
        "cotangent": bell_draw(own_keys[6], (NLAT, NLON, C), 1.0, 6.0, ((0, 2), (1, 8))),
    }


def far_table(psi_far, blocks):
    block_ids = jnp.arange(NBLK, dtype=jnp.int32)
    picker = (blocks[:, :, None] == block_ids[None, None, :]).astype(jnp.float32)
    dense_table = jnp.einsum('psb,pskwe->pkwbe', picker, psi_far.astype(jnp.float32))
    return dense_table.reshape(P_SIZE, K, 3, NLON).astype(jnp.bfloat16)

def reference(fields, psi_near, psi_far, blocks, weight, out_bias, cotangent):
    weight_f = weight.astype(jnp.float32)
    dense_table = far_table(psi_far, blocks).astype(jnp.float32)
    lon_ids = jnp.arange(NLON, dtype=jnp.int32)
    offsets = (lon_ids[None, :] - lon_ids[:, None]) % NLON
    padded_fields = jnp.pad(fields, ((1, 1), (0, 0), (0, 0)))
    polar_dz = lax.optimization_barrier(jnp.einsum('ijd,kcd->ijkc', cotangent[:P_SIZE].astype(jnp.float32), weight_f).astype(jnp.bfloat16))
    far_parts = []
    far_dx = jnp.zeros((P_SIZE + 2, NLON, C), jnp.float32)
    for polar_row in range(P_SIZE):
        circulant = dense_table[polar_row][:, :, offsets]
        near_rows = padded_fields[polar_row:polar_row + 3].astype(jnp.float32)
        far_parts.append(jnp.einsum('kwjm,wmc->jkc', circulant, near_rows))
        spread = jnp.einsum('kwjm,jkc->wmc', circulant, polar_dz[polar_row].astype(jnp.float32))
        far_dx = far_dx.at[polar_row:polar_row + 3].add(spread)
    far_z = jnp.stack(far_parts)
    far_dx = far_dx[1:]
    g_pad = jnp.pad(cotangent, ((0, 1), (0, 0), (0, 0)))
    psi_pad = jnp.pad(psi_near.astype(jnp.float32), ((1, 1), (0, 0), (0, 0), (0, 0)))

    def dz_row(row_index):
        g_row = lax.dynamic_index_in_dim(g_pad, row_index, 0, keepdims=False).astype(jnp.float32)
        return lax.optimization_barrier(jnp.einsum('md,kcd->mkc', g_row, weight_f).astype(jnp.bfloat16))

    def row_step(row_carry, row_index):
        dz_prev, dz_cur, grad_w, grad_b = row_carry
        dz_next = dz_row(row_index + 1)
        x_rows = lax.dynamic_slice_in_dim(padded_fields, row_index, 3, 0).astype(jnp.float32)
        psi_rows = lax.dynamic_slice_in_dim(psi_pad, row_index, 3, 0)
        z_sum = jnp.zeros((NLON, K, C), jnp.float32)
        for tap_row in range(3):
            for tap_col in range(3):
                shifted = jnp.roll(x_rows[tap_row], 1 - tap_col, axis=0)
                z_sum = z_sum + psi_rows[1, :, tap_row, tap_col][None, :, None] * shifted[:, None, :]
        far_here = lax.dynamic_index_in_dim(far_z, jnp.minimum(row_index, P_SIZE - 1), 0, keepdims=False)
        z_sum = z_sum + jnp.where(row_index < P_SIZE, far_here, 0.0)
        z_row = lax.optimization_barrier(z_sum.astype(jnp.bfloat16)).astype(jnp.float32)
        g_row = lax.dynamic_index_in_dim(g_pad, row_index, 0, keepdims=False).astype(jnp.float32)
        out_row = (jnp.einsum('mkc,kcd->md', z_row, weight_f) + out_bias).astype(jnp.bfloat16)
        grad_w = grad_w + jnp.einsum('mkc,md->kcd', z_row, g_row)
        grad_b = grad_b + lax.optimization_barrier(jnp.sum(g_row, axis=0))
        dz_list = (dz_next, dz_cur, dz_prev)
        dx_sum = jnp.zeros((NLON, C), jnp.float32)
        for tap_row in range(3):
            dz_f = dz_list[tap_row].astype(jnp.float32)
            for tap_col in range(3):
                shifted = jnp.roll(dz_f, tap_col - 1, axis=0)
                dx_sum = dx_sum + jnp.einsum('k,mkc->mc', psi_rows[2 - tap_row, :, tap_row, tap_col], shifted)
        far_back = lax.dynamic_index_in_dim(far_dx, jnp.minimum(row_index, P_SIZE), 0, keepdims=False)
        dx_sum = dx_sum + jnp.where(row_index <= P_SIZE, far_back, 0.0)
        return ((dz_cur, dz_next, grad_w, grad_b), (out_row, dx_sum.astype(jnp.bfloat16)))
    start_carry = (jnp.zeros((NLON, K, C), jnp.bfloat16), dz_row(jnp.int32(0)), jnp.zeros((K, C, C), jnp.float32), jnp.zeros((C,), jnp.float32))
    final_carry, row_outputs = lax.scan(row_step, start_carry, jnp.arange(NLAT, dtype=jnp.int32))
    out_rows, dx_rows = row_outputs
    grad_scale = 1.0 / math.sqrt(NLAT * NLON)
    return (out_rows, dx_rows, final_carry[2] * grad_scale, final_carry[3] * grad_scale)
```

```python
import functools
import math

import jax
import jax.numpy as jnp
from jax import lax
from jax.experimental import pallas as pl
from jax.experimental.pallas import tpu as pltpu
from jax.sharding import PartitionSpec as P

F32 = jnp.float32
BF16 = jnp.bfloat16
MESH = pl.DeviceIdType.MESH
BR = 8
FROWS = 6
CROWS = 4
GROUP = 8


def dot(a, b):
    return jnp.dot(a, b, preferred_element_type=F32)


def kernel(
    n, nrow, nl, kk, scale,
    x_ref, g_ref, e_ref, p_ref, t_ref, w_ref, b_ref,
    out_ref, gf_ref, gw_ref, gb_ref,
    hal, polf, polc, a_own, a_lr, a_t, a_j, a_farf, a_farc, zs, edge_acc,
    s0, r0, own, s1, r1, s2, r2, bsend, brecv,
    h_send, h_recv, p_send, p_recv, send0, recv0, send1, recv1, send2, recv2, b_ssem, b_rsem,
):
    part = lax.axis_index("parts")
    lat = lax.axis_index("lat")
    lon = lax.axis_index("lon")
    other = 1 - lat
    chan = x_ref.shape[1]
    half = chan // 2
    circle = n * nl
    nb = nrow // BR
    m = BR * nl * kk
    cells = BR * nl
    right = lax.rem(lon + 1, n)
    left = lax.rem(lon + n - 1, n)
    mine = lat * n + lon
    par = lax.rem(lon, 2)
    zz = lon // 2
    nz = n // 2
    rcp = pltpu.make_async_remote_copy

    barrier = pltpu.get_barrier_semaphore()

    def greet(step, _):
        to = lax.rem(mine + step, 2 * n)
        pl.semaphore_signal(
            barrier, inc=1, device_id=(part, to // n, lax.rem(to, n)), device_id_type=MESH
        )
        return 0

    lax.fori_loop(1, 2 * n, greet, 0)
    bsend[...] = jnp.broadcast_to(
        jnp.sum(g_ref[...].astype(F32), axis=0, keepdims=True), bsend.shape
    )
    pl.semaphore_wait(barrier, 2 * n - 1)

    srcs = (x_ref, g_ref)
    cut = pl.multiple_of(other * (nrow - 16), 16)
    cell_cut = pl.multiple_of(other * (nrow * nl - 16), 16)
    halo = []
    for d in range(2):
        first = e_ref.at[2 * d]
        last = e_ref.at[2 * d + 1]
        moves = (
            (last, 0, nrow, (part, lat, right)),
            (first, nrow, nrow, (part, lat, left)),
            (last.at[pl.ds(cut, 16)], 2 * nrow, 16, (part, other, right)),
            (first.at[pl.ds(cut, 16)], 2 * nrow + 16, 16, (part, other, left)),
            (srcs[d].at[pl.ds(cell_cut, 16)], 2 * nrow + 32, 16, (part, other, lon)),
        )
        for s, (src, start, size, to) in enumerate(moves):
            halo.append(
                rcp(
                    src_ref=src, dst_ref=hal.at[d, pl.ds(start, size)],
                    send_sem=h_send.at[d, s], recv_sem=h_recv.at[d, s],
                    device_id=to, device_id_type=MESH,
                )
            )

    def polar_copy(step, d):
        to = lax.rem(lon + step, n)
        buf, rows = ((polf, FROWS * nl), (polc, CROWS * nl))[d]
        return rcp(
            src_ref=srcs[d].at[pl.ds(0, rows)], dst_ref=buf.at[lon],
            send_sem=p_send.at[d, step], recv_sem=p_recv.at[d, step],
            device_id=(part, lat, to), device_id_type=MESH,
        )

    def bias_copy(step):
        to = lax.rem(mine + step, 2 * n)
        return rcp(
            src_ref=bsend, dst_ref=brecv.at[mine],
            send_sem=b_ssem.at[step], recv_sem=b_rsem.at[step],
            device_id=(part, to // n, lax.rem(to, n)), device_id_type=MESH,
        )

    def loop(lo, hi, body):
        def run(i, _):
            body(i)
            return 0

        lax.fori_loop(lo, hi, run, 0)

    for c in halo:
        c.start()

    @pl.when(lat == 0)
    def _():
        loop(1, n, lambda step: [polar_copy(step, d).start() for d in range(2)])
        polf[lon] = x_ref[0 : FROWS * nl, :]
        polc[lon] = g_ref[0 : CROWS * nl, :]

    loop(1, 2 * n, lambda step: bias_copy(step).start())
    brecv[mine] = bsend[...]

    def taps(b, rs, ls, qs, width):
        rid = lax.broadcasted_iota(jnp.int32, (m, width), 0)
        j = lax.rem(rid, nl)
        i = lax.rem(rid // nl, BR) + b * BR
        dr = rs - i + 1
        dl = ls - j + 1
        ok = (dr >= 0) & (dr < 3) & (dl >= 0) & (dl < 3)
        code = jnp.where(ok, dr * 3 + dl, -1)
        start = b * m if isinstance(b, int) else pl.multiple_of(b * m, m)
        coefs = p_ref[pl.ds(start, m), :]
        fwd = jnp.zeros((m, width), F32)
        bwd = jnp.zeros((m, width), F32)
        for q in qs:
            hit = code == q
            fwd = jnp.where(hit, coefs[:, q : q + 1], fwd)
            bwd = jnp.where(hit, coefs[:, 17 - q : 18 - q], bwd)
        return fwd.astype(BF16), bwd.astype(BF16)

    def window(b):
        return jnp.clip(b * BR - 4, 0, nrow - 16)

    def build(b):
        lane = lax.broadcasted_iota(jnp.int32, (m, 16 * nl), 1)
        a_own[0, b], a_own[1, b] = taps(
            b, window(b) + lane // nl, lax.rem(lane, nl), range(9), 16 * nl
        )
        lane = lax.broadcasted_iota(jnp.int32, (m, 2 * nrow), 1)
        a_lr[0, b], a_lr[1, b] = taps(
            b, lax.rem(lane, nrow), jnp.where(lane < nrow, -1, nl), (0, 2, 3, 5, 6, 8), 2 * nrow
        )

    loop(0, nb, build)
    lane = lax.broadcasted_iota(jnp.int32, (m, 48), 1)
    rs = jnp.where(
        lane < 32,
        lax.rem(lane, 16) + jnp.where(lat == 0, nrow, -16),
        (lane - 32) // nl + jnp.where(lat == 0, nrow, -16 // nl),
    )
    ls = jnp.where(lane < 16, -1, jnp.where(lane < 32, nl, lax.rem(lane, nl)))
    a_t[0], a_t[1] = taps(other * (nb - 1), rs, ls, range(9), 48)

    tr = kk * BR

    @pl.when(lat == 0)
    def _():
        rid = lax.broadcasted_iota(jnp.int32, (m, m), 0)
        cid = lax.broadcasted_iota(jnp.int32, (m, m), 1)
        order = ((rid // nl == lax.rem(cid, tr)) & (lax.rem(rid, nl) == cid // tr)).astype(BF16)
        for d, rows in ((0, FROWS), (1, CROWS)):
            wide = GROUP * rows * nl

            def far_group(grp, d=d, rows=rows, wide=wide):
                lane = lax.broadcasted_iota(jnp.int32, (circle, wide), 1)
                t_id = lax.broadcasted_iota(jnp.int32, (circle, wide), 0)
                lon_of = (grp * GROUP + lane // (rows * nl)) * nl + lax.rem(lane, nl)
                rlane = lax.broadcasted_iota(jnp.int32, (tr, wide), 1)
                r_of = lax.rem(rlane // nl, rows)
                i_of = lax.rem(lax.broadcasted_iota(jnp.int32, (tr, wide), 0), BR)
                dist = lon_of - lon * nl + circle
                for j in range(nl):
                    if d == 0:
                        t_want = lax.rem(dist - j + circle, circle)
                    else:
                        t_want = lax.rem(2 * circle - dist + j + circle, circle)
                    pick = (t_id == t_want).astype(BF16)
                    full = dot(t_ref[d * 3 * tr : (d + 1) * 3 * tr, :], pick)
                    acc = jnp.zeros((tr, wide), F32)
                    for w in range(3):
                        hit = (r_of - i_of + 1 == w) if d == 0 else (i_of - r_of + 1 == w)
                        acc = jnp.where(hit, full[w * tr : (w + 1) * tr], acc)
                    a_j[j * tr : (j + 1) * tr, 0:wide] = acc.astype(BF16)
                dst = a_farf if d == 0 else a_farc
                dst[grp] = dot(order, a_j[:, 0:wide]).astype(BF16)

            loop(0, n // GROUP, far_group)

    def near(d, b):
        start = window(b) * nl
        start = pl.multiple_of(start, 16)
        return dot(a_own[d, b], srcs[d][pl.ds(start, 16 * nl), :]) + dot(
            a_lr[d, b], hal[d, 0 : 2 * nrow, :]
        )

    def put(d, b, acc):
        at = pl.multiple_of(b * cells, cells)
        for k in range(kk):
            zs[d, k, pl.ds(at, cells), :] = acc[k * cells : (k + 1) * cells].astype(BF16)

    def inner(d):
        loop(1, nb - 1, lambda b: put(d, b, near(d, b)))

    def edges(d):
        edge_acc[0] = near(d, jnp.int32(0))
        edge_acc[1] = near(d, jnp.int32(nb - 1))
        edge_acc[other] += dot(a_t[d], hal[d, 2 * nrow : 2 * nrow + 48, :])

        @pl.when(lat == 0)
        def _():
            loop(1, n, lambda step: polar_copy(step, d).wait())
            buf, coefs, rows = ((polf, a_farf, FROWS), (polc, a_farc, CROWS))[d]

            def far_add(grp):
                src = buf[pl.ds(grp * GROUP, GROUP)].reshape(GROUP * rows * nl, chan)
                edge_acc[0] += dot(coefs[grp], src)

            loop(0, n // GROUP, far_add)

        put(d, jnp.int32(0), edge_acc[0])
        put(d, jnp.int32(nb - 1), edge_acc[1])

    for c in halo:
        c.wait()
    inner(0)
    edges(0)

    def copy0(k):
        return rcp(
            src_ref=s0.at[k], dst_ref=r0.at[k], send_sem=send0.at[k], recv_sem=recv0.at[k],
            device_id=(part, other, lon), device_id_type=MESH,
        )

    def copy1(k):
        return rcp(
            src_ref=s1.at[k], dst_ref=r1.at[k], send_sem=send1.at[k], recv_sem=recv1.at[k],
            device_id=(part, lat, lon + 1 - 2 * par), device_id_type=MESH,
        )

    def copy2(k, step):
        to = lax.rem(zz + step, nz)
        return rcp(
            src_ref=s2.at[k, to], dst_ref=r2.at[k, zz],
            send_sem=send2.at[k, step], recv_sem=recv2.at[k, step],
            device_id=(part, lat, to * 2 + par), device_id_type=MESH,
        )

    def grads(k, which):
        z = zs[0, k, :, pl.ds(pl.multiple_of(which * half, half), half)]
        return lax.dot_general(
            z, g_ref[...], (((0,), (0,)), ((), ())), preferred_element_type=F32
        )

    def stage0(k):
        s0[k] = grads(k, other).astype(BF16)
        copy0(k).start()

    def keep(k):
        own[k] = grads(k, lat).reshape(own.shape[1:])

    loop(0, kk, stage0)
    loop(0, kk, keep)

    def stage1(k):
        copy0(k).wait()
        own[k] += r0[k].astype(F32).reshape(own.shape[1:])
        for q in range(nz):
            s1[k, q] = own[k, q, 1 - par].astype(BF16)
        copy1(k).start()

    loop(0, kk, stage1)

    step_rows = 256

    def forward(b):
        at = pl.ds(pl.multiple_of(b * step_rows, step_rows), step_rows)
        acc = dot(zs[0, 0, at, :], w_ref[0])
        for k in range(1, kk):
            acc += dot(zs[0, k, at, :], w_ref[k])
        out_ref[at, :] = (acc + b_ref[...]).astype(BF16)

    loop(0, nrow * nl // step_rows, forward)

    def stage2(k):
        copy1(k).wait()
        for q in range(nz):
            own[k, q, par] += r1[k, q].astype(F32)
            s2[k, q] = own[k, q, par].astype(BF16)
        loop(1, nz, lambda step: copy2(k, step).start())

    loop(0, kk, stage2)

    inner(1)
    edges(1)

    def backward(b):
        at = pl.ds(pl.multiple_of(b * step_rows, step_rows), step_rows)
        acc = None
        for k in range(kk):
            term = lax.dot_general(
                zs[1, k, at, :], w_ref[k], (((1,), (1,)), ((), ())), preferred_element_type=F32
            )
            acc = term if acc is None else acc + term
        gf_ref[at, :] = acc.astype(BF16)

    loop(0, nrow * nl // step_rows, backward)

    loop(1, 2 * n, lambda step: bias_copy(step).wait())
    gb_ref[...] = jnp.sum(brecv[...], axis=0) * scale

    def final(k):
        gw_ref[k] = own[k, zz, par]

        def take(step):
            copy2(k, step).wait()
            gw_ref[k] += r2[k, lax.rem(zz + nz - step, nz)].astype(F32)

        loop(1, nz, take)
        gw_ref[k] = gw_ref[k] * scale

    loop(0, kk, final)


def on_device(fields, psi_near, psi_far, blocks, weight, out_bias, cotangent):
    nrow, nl, chan = fields.shape
    kk = weight.shape[0]
    npol, ns, _, _, bw = psi_far.shape
    n = lax.axis_size("lon")
    circle = n * nl
    lat = lax.axis_index("lat")
    nb = nrow // BR
    m = BR * nl * kk

    psi_pad = jnp.pad(psi_near, ((1, 1), (0, 0), (0, 0), (0, 0)))
    psi = lax.dynamic_slice_in_dim(psi_pad, lat * nrow, nrow + 2, 0)
    own_rows = psi[1 : nrow + 1].reshape(nrow, kk, 9)
    back = [psi[2 - w : 2 - w + nrow, :, w] for w in range(3)]
    both = jnp.concatenate([own_rows] + back, axis=2)
    both = both.reshape(nb, BR, kk, 18).transpose(0, 2, 1, 3).astype(F32)
    coefs = jnp.broadcast_to(both[:, :, :, None, :], (nb, kk, BR, nl, 18)).reshape(nb * m, 18)

    ids = jnp.arange(circle // bw, dtype=jnp.int32)
    picker = (blocks[:, :, None] == ids).astype(BF16)
    table = jnp.einsum("psb,pskwe->wkpbe", picker, psi_far, preferred_element_type=F32)
    table = table.reshape(3, kk, npol, circle).astype(BF16)
    tf = jnp.pad(table, ((0, 0), (0, 0), (0, BR - npol), (0, 0)))
    wide = jnp.pad(table, ((0, 0), (0, 0), (1, BR), (0, 0)))
    tb = jnp.stack([wide[w, :, 2 - w : 2 - w + BR] for w in range(3)])
    tables = jnp.concatenate([tf, tb]).reshape(6 * kk * BR, circle)

    edge_cols = jnp.stack([fields[:, 0], fields[:, nl - 1], cotangent[:, 0], cotangent[:, nl - 1]])
    lat_count = lax.axis_size("lat")
    scale = 1.0 / math.sqrt(nrow * lat_count * circle)
    nz = n // 2
    cr = chan // 2 // n
    vmem = pl.BlockSpec(memory_space=pltpu.VMEM)
    dma = pltpu.SemaphoreType.DMA
    ng = n // GROUP
    out, gf, gw, gb = pl.pallas_call(
        functools.partial(kernel, n, nrow, nl, kk, scale),
        out_shape=(
            jax.ShapeDtypeStruct((nrow * nl, chan), BF16),
            jax.ShapeDtypeStruct((nrow * nl, chan), BF16),
            jax.ShapeDtypeStruct((kk, cr, chan), F32),
            jax.ShapeDtypeStruct((8, chan), F32),
        ),
        in_specs=[vmem] * 7,
        out_specs=(vmem,) * 4,
        scratch_shapes=[
            pltpu.VMEM((2, 2 * nrow + 48, chan), BF16),
            pltpu.VMEM((n, FROWS * nl, chan), BF16),
            pltpu.VMEM((n, CROWS * nl, chan), BF16),
            pltpu.VMEM((2, nb, m, 16 * nl), BF16),
            pltpu.VMEM((2, nb, m, 2 * nrow), BF16),
            pltpu.VMEM((2, m, 48), BF16),
            pltpu.VMEM((m, GROUP * FROWS * nl), BF16),
            pltpu.VMEM((ng, m, GROUP * FROWS * nl), BF16),
            pltpu.VMEM((ng, m, GROUP * CROWS * nl), BF16),
            pltpu.VMEM((2, kk, nrow * nl, chan), BF16),
            pltpu.VMEM((2, m, chan), F32),
            pltpu.VMEM((kk, chan // 2, chan), BF16),
            pltpu.VMEM((kk, chan // 2, chan), BF16),
            pltpu.VMEM((kk, nz, 2, cr, chan), F32),
            pltpu.VMEM((kk, nz, cr, chan), BF16),
            pltpu.VMEM((kk, nz, cr, chan), BF16),
            pltpu.VMEM((kk, nz, cr, chan), BF16),
            pltpu.VMEM((kk, nz, cr, chan), BF16),
            pltpu.VMEM((8, chan), F32),
            pltpu.VMEM((2 * n, 8, chan), F32),
            dma((2, 5)), dma((2, 5)),
            dma((2, n)), dma((2, n)),
            dma((kk,)), dma((kk,)),
            dma((kk,)), dma((kk,)),
            dma((kk, nz)), dma((kk, nz)),
            dma((2 * n,)), dma((2 * n,)),
        ],
        compiler_params=pltpu.CompilerParams(
            collective_id=0, has_side_effects=True, vmem_limit_bytes=56 * 1024 * 1024
        ),
        cost_estimate=pl.CostEstimate(
            flops=8 * nrow * nl * kk * chan * chan, bytes_accessed=8 << 20, transcendentals=0
        ),
    )(
        fields.reshape(nrow * nl, chan),
        cotangent.reshape(nrow * nl, chan),
        edge_cols, coefs, tables, weight, out_bias.reshape(1, chan),
    )
    place = lat * n + lax.axis_index("lon")
    share = chan // (lat_count * n)
    grad_bias = lax.dynamic_slice_in_dim(gb[0], place * share, share, 0)
    return (out.reshape(fields.shape), gf.reshape(fields.shape), gw, grad_bias)


def solution(mesh):
    return jax.shard_map(
        on_device,
        mesh=mesh,
        in_specs=(
            P(("parts", "lat"), "lon", None), P(), P(), P(), P(), P(),
            P(("parts", "lat"), "lon", None),
        ),
        out_specs=(
            P(("parts", "lat"), "lon", None),
            P(("parts", "lat"), "lon", None),
            P(None, ("parts", "lat", "lon"), None),
            P(("parts", "lat", "lon")),
        ),
        check_vma=False,
    )
```

```python
import functools
import math

import jax
import jax.numpy as jnp
from jax import lax
from jax.experimental import pallas as pl
from jax.experimental.pallas import tpu as pltpu
from jax.sharding import PartitionSpec as P

F32 = jnp.float32
BF16 = jnp.bfloat16
MESH = pl.DeviceIdType.MESH
BR = 8
FROWS = 6
CROWS = 4
GROUP = 8


def dot(a, b):
    return jnp.dot(a, b, preferred_element_type=F32)


def kernel(
    n, nrow, nl, kk, scale,
    x_ref, g_ref, psi_ref, far_ref, blk_ref, w_hbm, b_ref,
    out_hbm, gf_hbm, gw_ref, gb_ref,
    w_ref, out_ref, gf_ref, ecols, t_ref, loc_sem,
    hal, polf, polc, a_own, a_lr, a_t, a_j, a_farf, a_farc, zs, edge_acc,
    s0, r0, own, s1, r1, s2, r2, bsend, brecv,
    h_send, h_recv, p_send, p_recv, send0, recv0, send1, recv1, send2, recv2, b_ssem, b_rsem,
):
    part = lax.axis_index("parts")
    lat = lax.axis_index("lat")
    lon = lax.axis_index("lon")
    other = 1 - lat
    chan = x_ref.shape[1]
    half = chan // 2
    circle = n * nl
    nb = nrow // BR
    m = BR * nl * kk
    cells = BR * nl
    right = lax.rem(lon + 1, n)
    left = lax.rem(lon + n - 1, n)
    mine = lat * n + lon
    par = lax.rem(lon, 2)
    zz = lon // 2
    nz = n // 2
    rcp = pltpu.make_async_remote_copy
    load_w = pltpu.make_async_copy(w_hbm, w_ref, loc_sem.at[0])
    store_out = pltpu.make_async_copy(out_ref, out_hbm, loc_sem.at[1])
    store_gf = pltpu.make_async_copy(gf_ref, gf_hbm, loc_sem.at[2])
    load_w.start()

    barrier = pltpu.get_barrier_semaphore()

    def greet(step, _):
        to = lax.rem(mine + step, 2 * n)
        pl.semaphore_signal(
            barrier, inc=1, device_id=(part, to // n, lax.rem(to, n)), device_id_type=MESH
        )
        return 0

    lax.fori_loop(1, 2 * n, greet, 0)
    bsend[...] = jnp.broadcast_to(
        jnp.sum(g_ref[...].astype(F32), axis=0, keepdims=True), bsend.shape
    )
    rid = lax.broadcasted_iota(jnp.int32, (2 * nrow, nrow * nl), 0)
    cid = lax.broadcasted_iota(jnp.int32, (2 * nrow, nrow * nl), 1)
    want = lax.rem(rid, nrow) * nl + jnp.where(rid < nrow, 0, nl - 1)
    ends = (cid == want).astype(BF16)
    for d, src in enumerate((x_ref, g_ref)):
        picked = dot(ends, src[...]).astype(BF16)
        ecols[2 * d] = picked[:nrow]
        ecols[2 * d + 1] = picked[nrow:]
    pl.semaphore_wait(barrier, 2 * n - 1)

    srcs = (x_ref, g_ref)
    cut = pl.multiple_of(other * (nrow - 16), 16)
    cell_cut = pl.multiple_of(other * (nrow * nl - 16), 16)
    halo = []
    for d in range(2):
        first = ecols.at[2 * d]
        last = ecols.at[2 * d + 1]
        moves = (
            (last, 0, nrow, (part, lat, right)),
            (first, nrow, nrow, (part, lat, left)),
            (last.at[pl.ds(cut, 16)], 2 * nrow, 16, (part, other, right)),
            (first.at[pl.ds(cut, 16)], 2 * nrow + 16, 16, (part, other, left)),
            (srcs[d].at[pl.ds(cell_cut, 16)], 2 * nrow + 32, 16, (part, other, lon)),
        )
        for s, (src, start, size, to) in enumerate(moves):
            halo.append(
                rcp(
                    src_ref=src, dst_ref=hal.at[d, pl.ds(start, size)],
                    send_sem=h_send.at[d, s], recv_sem=h_recv.at[d, s],
                    device_id=to, device_id_type=MESH,
                )
            )

    def polar_copy(step, d):
        to = lax.rem(lon + step, n)
        buf, rows = ((polf, FROWS * nl), (polc, CROWS * nl))[d]
        return rcp(
            src_ref=srcs[d].at[pl.ds(0, rows)], dst_ref=buf.at[lon],
            send_sem=p_send.at[d, step], recv_sem=p_recv.at[d, step],
            device_id=(part, lat, to), device_id_type=MESH,
        )

    def bias_copy(step):
        to = lax.rem(mine + step, 2 * n)
        return rcp(
            src_ref=bsend, dst_ref=brecv.at[mine],
            send_sem=b_ssem.at[step], recv_sem=b_rsem.at[step],
            device_id=(part, to // n, lax.rem(to, n)), device_id_type=MESH,
        )

    def loop(lo, hi, body):
        def run(i, _):
            body(i)
            return 0

        lax.fori_loop(lo, hi, run, 0)

    for c in halo:
        c.start()

    @pl.when(lat == 0)
    def _():
        loop(1, n, lambda step: [polar_copy(step, d).start() for d in range(2)])
        polf[lon] = x_ref[0 : FROWS * nl, :]
        polc[lon] = g_ref[0 : CROWS * nl, :]

    loop(1, 2 * n, lambda step: bias_copy(step).start())
    brecv[mine] = bsend[...]

    nlat = psi_ref.shape[1]

    def psi_rows(b):
        rid = lax.broadcasted_iota(jnp.int32, (3 * cells, nlat), 0)
        cid = lax.broadcasted_iota(jnp.int32, (3 * cells, nlat), 1)
        want = lat * nrow + b * BR + lax.rem(rid, cells) // nl + 1 - rid // cells
        return lax.dot_general(
            (cid == want).astype(BF16), psi_ref[...], (((1,), (1,)), ((), ())),
            preferred_element_type=F32,
        )

    def taps(b, pv, rs, ls, qs, dst):
        width = rs.shape[1]
        rid = lax.broadcasted_iota(jnp.int32, (cells, width), 0)
        dr = rs - (rid // nl + b * BR) + 1
        dl = ls - lax.rem(rid, nl) + 1
        ok = (dr >= 0) & (dr < 3) & (dl >= 0) & (dl < 3)
        code = jnp.where(ok, dr * 3 + dl, -1)
        for d in range(2):
            for k in range(kk):
                vals = jnp.zeros((cells, width), F32)
                for q in qs:
                    w, at = (1, q * kk + k) if d == 0 else (2 - q // 3, (8 - q) * kk + k)
                    col = pv[w * cells : (w + 1) * cells, at : at + 1]
                    vals = jnp.where(code == q, col, vals)
                dst(d, k, vals.astype(BF16))

    def window(b):
        return jnp.clip(b * BR - 4, 0, nrow - 16)

    def build(b):
        pv = psi_rows(b)

        def put_own(d, k, vals):
            a_own[d, b, k * cells : (k + 1) * cells, :] = vals

        def put_lr(d, k, vals):
            a_lr[d, b, k * cells : (k + 1) * cells, :] = vals

        lane = lax.broadcasted_iota(jnp.int32, (cells, 16 * nl), 1)
        taps(b, pv, window(b) + lane // nl, lax.rem(lane, nl), range(9), put_own)
        lane = lax.broadcasted_iota(jnp.int32, (cells, 2 * nrow), 1)
        taps(
            b, pv, lax.rem(lane, nrow), jnp.where(lane < nrow, -1, nl), (0, 2, 3, 5, 6, 8), put_lr
        )

    loop(0, nb, build)
    lane = lax.broadcasted_iota(jnp.int32, (cells, 48), 1)
    rs = jnp.where(
        lane < 32,
        lax.rem(lane, 16) + jnp.where(lat == 0, nrow, -16),
        (lane - 32) // nl + jnp.where(lat == 0, nrow, -16 // nl),
    )
    ls = jnp.where(lane < 16, -1, jnp.where(lane < 32, nl, lax.rem(lane, nl)))

    def put_t(d, k, vals):
        a_t[d, k * cells : (k + 1) * cells, :] = vals

    eb = other * (nb - 1)
    taps(eb, psi_rows(eb), rs, ls, range(9), put_t)

    tr = kk * BR

    @pl.when(lat == 0)
    def _():
        rid = lax.broadcasted_iota(jnp.int32, (m, m), 0)
        cid = lax.broadcasted_iota(jnp.int32, (m, m), 1)
        frows, bw = far_ref.shape
        npol, ns = blk_ref.shape
        lane = lax.broadcasted_iota(jnp.int32, (bw, circle), 1)
        spread = (lax.broadcasted_iota(jnp.int32, (bw, circle), 0) == lax.rem(lane, bw)).astype(BF16)
        frow = lax.broadcasted_iota(jnp.int32, (frows, circle), 0) // (3 * kk)
        block = jnp.zeros((frows, circle), jnp.int32)
        for q in range(npol * ns):
            block = jnp.where(frow == q, blk_ref[q // ns, q % ns], block)
        lane = lax.broadcasted_iota(jnp.int32, (frows, circle), 1)
        named = jnp.where(block == lane // bw, dot(far_ref[...], spread), 0.0).astype(BF16)
        trow = lax.broadcasted_iota(jnp.int32, (6 * tr, frows), 0)
        srow = lax.broadcasted_iota(jnp.int32, (6 * tr, frows), 1)
        t_i = lax.rem(trow, BR)
        t_wk = lax.rem(trow, 3 * tr) // BR
        t_p = jnp.where(trow < 3 * tr, t_i, t_i - t_wk // kk + 1)
        pick_row = (lax.rem(srow, 3 * kk) == t_wk) & (srow // (3 * kk * ns) == t_p)
        t_ref[...] = dot(pick_row.astype(BF16), named).astype(BF16)
        order = ((rid // nl == lax.rem(cid, tr)) & (lax.rem(rid, nl) == cid // tr)).astype(BF16)
        for d, rows in ((0, FROWS), (1, CROWS)):
            wide = GROUP * rows * nl

            def far_group(grp, d=d, rows=rows, wide=wide):
                lane = lax.broadcasted_iota(jnp.int32, (circle, wide), 1)
                t_id = lax.broadcasted_iota(jnp.int32, (circle, wide), 0)
                lon_of = (grp * GROUP + lane // (rows * nl)) * nl + lax.rem(lane, nl)
                rlane = lax.broadcasted_iota(jnp.int32, (tr, wide), 1)
                r_of = lax.rem(rlane // nl, rows)
                i_of = lax.rem(lax.broadcasted_iota(jnp.int32, (tr, wide), 0), BR)
                dist = lon_of - lon * nl + circle
                for j in range(nl):
                    if d == 0:
                        t_want = lax.rem(dist - j + circle, circle)
                    else:
                        t_want = lax.rem(2 * circle - dist + j + circle, circle)
                    pick = (t_id == t_want).astype(BF16)
                    full = dot(t_ref[d * 3 * tr : (d + 1) * 3 * tr, :], pick)
                    acc = jnp.zeros((tr, wide), F32)
                    for w in range(3):
                        hit = (r_of - i_of + 1 == w) if d == 0 else (i_of - r_of + 1 == w)
                        acc = jnp.where(hit, full[w * tr : (w + 1) * tr], acc)
                    a_j[j * tr : (j + 1) * tr, 0:wide] = acc.astype(BF16)
                dst = a_farf if d == 0 else a_farc
                dst[grp] = dot(order, a_j[:, 0:wide]).astype(BF16)

            loop(0, n // GROUP, far_group)

    def near(d, b):
        start = window(b) * nl
        start = pl.multiple_of(start, 16)
        return dot(a_own[d, b], srcs[d][pl.ds(start, 16 * nl), :]) + dot(
            a_lr[d, b], hal[d, 0 : 2 * nrow, :]
        )

    def put(d, b, acc):
        at = pl.multiple_of(b * cells, cells)
        for k in range(kk):
            zs[d, k, pl.ds(at, cells), :] = acc[k * cells : (k + 1) * cells].astype(BF16)

    def inner(d):
        loop(1, nb - 1, lambda b: put(d, b, near(d, b)))

    def edges(d):
        edge_acc[0] = near(d, jnp.int32(0))
        edge_acc[1] = near(d, jnp.int32(nb - 1))
        edge_acc[other] += dot(a_t[d], hal[d, 2 * nrow : 2 * nrow + 48, :])

        @pl.when(lat == 0)
        def _():
            loop(1, n, lambda step: polar_copy(step, d).wait())
            buf, coefs, rows = ((polf, a_farf, FROWS), (polc, a_farc, CROWS))[d]

            def far_add(grp):
                src = buf[pl.ds(grp * GROUP, GROUP)].reshape(GROUP * rows * nl, chan)
                edge_acc[0] += dot(coefs[grp], src)

            loop(0, n // GROUP, far_add)

        put(d, jnp.int32(0), edge_acc[0])
        put(d, jnp.int32(nb - 1), edge_acc[1])

    for c in halo:
        c.wait()
    inner(0)
    edges(0)

    def copy0(k):
        return rcp(
            src_ref=s0.at[k], dst_ref=r0.at[k], send_sem=send0.at[k], recv_sem=recv0.at[k],
            device_id=(part, other, lon), device_id_type=MESH,
        )

    def copy1(k):
        return rcp(
            src_ref=s1.at[k], dst_ref=r1.at[k], send_sem=send1.at[k], recv_sem=recv1.at[k],
            device_id=(part, lat, lon + 1 - 2 * par), device_id_type=MESH,
        )

    def copy2(k, step):
        to = lax.rem(zz + step, nz)
        return rcp(
            src_ref=s2.at[k, to], dst_ref=r2.at[k, zz],
            send_sem=send2.at[k, step], recv_sem=recv2.at[k, step],
            device_id=(part, lat, to * 2 + par), device_id_type=MESH,
        )

    def grads(k, which):
        z = zs[0, k, :, pl.ds(pl.multiple_of(which * half, half), half)]
        return lax.dot_general(
            z, g_ref[...], (((0,), (0,)), ((), ())), preferred_element_type=F32
        )

    def stage0(k):
        s0[k] = grads(k, other).astype(BF16)
        copy0(k).start()

    def keep(k):
        own[k] = grads(k, lat).reshape(own.shape[1:])

    loop(0, kk, stage0)
    loop(0, kk, keep)

    def stage1(k):
        copy0(k).wait()
        own[k] += r0[k].astype(F32).reshape(own.shape[1:])
        for q in range(nz):
            s1[k, q] = own[k, q, 1 - par].astype(BF16)
        copy1(k).start()

    loop(0, kk, stage1)

    step_rows = 256

    def forward(b):
        at = pl.ds(pl.multiple_of(b * step_rows, step_rows), step_rows)
        acc = dot(zs[0, 0, at, :], w_ref[0])
        for k in range(1, kk):
            acc += dot(zs[0, k, at, :], w_ref[k])
        out_ref[at, :] = (acc + b_ref[...]).astype(BF16)

    load_w.wait()
    loop(0, nrow * nl // step_rows, forward)
    store_out.start()

    def stage2(k):
        copy1(k).wait()
        for q in range(nz):
            own[k, q, par] += r1[k, q].astype(F32)
            s2[k, q] = own[k, q, par].astype(BF16)
        loop(1, nz, lambda step: copy2(k, step).start())

    loop(0, kk, stage2)

    inner(1)
    edges(1)

    def backward(b):
        at = pl.ds(pl.multiple_of(b * step_rows, step_rows), step_rows)
        acc = None
        for k in range(kk):
            term = lax.dot_general(
                zs[1, k, at, :], w_ref[k], (((1,), (1,)), ((), ())), preferred_element_type=F32
            )
            acc = term if acc is None else acc + term
        gf_ref[at, :] = acc.astype(BF16)

    loop(0, nrow * nl // step_rows, backward)
    store_gf.start()

    loop(1, 2 * n, lambda step: bias_copy(step).wait())
    gb_ref[...] = jnp.sum(brecv[...], axis=0) * scale

    def final(k):
        gw_ref[k] = own[k, zz, par]

        def take(step):
            copy2(k, step).wait()
            gw_ref[k] += r2[k, lax.rem(zz + nz - step, nz)].astype(F32)

        loop(1, nz, take)
        gw_ref[k] = gw_ref[k] * scale

    loop(0, kk, final)
    store_out.wait()
    store_gf.wait()


def hand_on(n, out_in, gf_in, gw_in, gb_in, out_ref, gf_ref, gw_ref, gb_ref, sem):
    copies = []
    for a, (src, dst) in enumerate(((out_in, out_ref), (gf_in, gf_ref), (gw_in, gw_ref))):
        count = sem.shape[1]
        size = src.shape[0] // count
        for c in range(count):
            at = pl.ds(c * size, size)
            copies.append(pltpu.make_async_copy(src.at[at], dst.at[at], sem.at[a, c]))
    for c in copies:
        c.start()
    share = gb_ref.shape[1]
    chan = gb_in.shape[1]
    place = lax.axis_index("lat") * n + lax.axis_index("lon")
    gb_ref[...] = pltpu.roll(gb_in[...], lax.rem(chan - place * share, chan), 1)[0:1, :share]
    for c in copies:
        c.wait()


def on_device(fields, psi_near, psi_far, blocks, weight, out_bias, cotangent):
    nrow, nl, chan = fields.shape
    kk = weight.shape[0]
    npol, ns, _, _, bw = psi_far.shape
    n = lax.axis_size("lon")
    circle = n * nl
    nb = nrow // BR
    m = BR * nl * kk
    taps = psi_near.transpose(2, 3, 1, 0).reshape(9 * kk, psi_near.shape[0])
    far = psi_far.transpose(0, 1, 3, 2, 4).reshape(npol * ns * 3 * kk, bw)
    lat_count = lax.axis_size("lat")
    scale = 1.0 / math.sqrt(nrow * lat_count * circle)
    nz = n // 2
    cr = chan // 2 // n
    vmem = pl.BlockSpec(memory_space=pltpu.VMEM)
    anywhere = pl.BlockSpec(memory_space=pl.ANY)
    dma = pltpu.SemaphoreType.DMA
    ng = n // GROUP
    out, gf, gw, gb = pl.pallas_call(
        functools.partial(kernel, n, nrow, nl, kk, scale),
        out_shape=(
            jax.ShapeDtypeStruct((nrow * nl, chan), BF16),
            jax.ShapeDtypeStruct((nrow * nl, chan), BF16),
            jax.ShapeDtypeStruct((kk, cr, chan), F32),
            jax.ShapeDtypeStruct((8, chan), F32),
        ),
        in_specs=[vmem] * 4 + [pl.BlockSpec(memory_space=pltpu.SMEM), anywhere, vmem],
        out_specs=(anywhere, anywhere, vmem, vmem),
        scratch_shapes=[
            pltpu.VMEM(weight.shape, BF16),
            pltpu.VMEM((nrow * nl, chan), BF16),
            pltpu.VMEM((nrow * nl, chan), BF16),
            pltpu.VMEM((4, nrow, chan), BF16),
            pltpu.VMEM((6 * kk * BR, circle), BF16),
            dma((3,)),
            pltpu.VMEM((2, 2 * nrow + 48, chan), BF16),
            pltpu.VMEM((n, FROWS * nl, chan), BF16),
            pltpu.VMEM((n, CROWS * nl, chan), BF16),
            pltpu.VMEM((2, nb, m, 16 * nl), BF16),
            pltpu.VMEM((2, nb, m, 2 * nrow), BF16),
            pltpu.VMEM((2, m, 48), BF16),
            pltpu.VMEM((m, GROUP * FROWS * nl), BF16),
            pltpu.VMEM((ng, m, GROUP * FROWS * nl), BF16),
            pltpu.VMEM((ng, m, GROUP * CROWS * nl), BF16),
            pltpu.VMEM((2, kk, nrow * nl, chan), BF16),
            pltpu.VMEM((2, m, chan), F32),
            pltpu.VMEM((kk, chan // 2, chan), BF16),
            pltpu.VMEM((kk, chan // 2, chan), BF16),
            pltpu.VMEM((kk, nz, 2, cr, chan), F32),
            pltpu.VMEM((kk, nz, cr, chan), BF16),
            pltpu.VMEM((kk, nz, cr, chan), BF16),
            pltpu.VMEM((kk, nz, cr, chan), BF16),
            pltpu.VMEM((kk, nz, cr, chan), BF16),
            pltpu.VMEM((8, chan), F32),
            pltpu.VMEM((2 * n, 8, chan), F32),
            dma((2, 5)), dma((2, 5)),
            dma((2, n)), dma((2, n)),
            dma((kk,)), dma((kk,)),
            dma((kk,)), dma((kk,)),
            dma((kk, nz)), dma((kk, nz)),
            dma((2 * n,)), dma((2 * n,)),
        ],
        compiler_params=pltpu.CompilerParams(
            collective_id=0, has_side_effects=True, vmem_limit_bytes=56 * 1024 * 1024
        ),
        cost_estimate=pl.CostEstimate(
            flops=8 * nrow * nl * kk * chan * chan, bytes_accessed=8 << 20, transcendentals=0
        ),
    )(
        fields.reshape(nrow * nl, chan),
        cotangent.reshape(nrow * nl, chan),
        taps, far, blocks, weight, out_bias.reshape(1, chan),
    )
    share = chan // (lat_count * n)
    out, gf, gw, gb = pl.pallas_call(
        functools.partial(hand_on, n),
        out_shape=(
            jax.ShapeDtypeStruct(out.shape, BF16),
            jax.ShapeDtypeStruct(gf.shape, BF16),
            jax.ShapeDtypeStruct(gw.shape, F32),
            jax.ShapeDtypeStruct((1, share), F32),
        ),
        in_specs=[anywhere] * 3 + [vmem],
        out_specs=(anywhere,) * 3 + (vmem,),
        scratch_shapes=[dma((3, kk))],
        compiler_params=pltpu.CompilerParams(vmem_limit_bytes=56 * 1024 * 1024),
    )(out, gf, gw, gb)
    return (out.reshape(fields.shape), gf.reshape(fields.shape), gw, gb.reshape(share))


def solution(mesh):
    return jax.shard_map(
        on_device,
        mesh=mesh,
        in_specs=(
            P(("parts", "lat"), "lon", None), P(), P(), P(), P(), P(),
            P(("parts", "lat"), "lon", None),
        ),
        out_specs=(
            P(("parts", "lat"), "lon", None),
            P(("parts", "lat"), "lon", None),
            P(None, ("parts", "lat", "lon"), None),
            P(("parts", "lat", "lon")),
        ),
        check_vma=False,
    )
```

```python
import functools
import math

import jax
import jax.numpy as jnp
from jax import lax
from jax.experimental import pallas as pl
from jax.experimental.pallas import tpu as pltpu
from jax.sharding import PartitionSpec as P

F32 = jnp.float32
BF16 = jnp.bfloat16
MESH = pl.DeviceIdType.MESH
BR = 8
FROWS = 6
CROWS = 4
GROUP = 8


def dot(a, b):
    return jnp.dot(a, b, preferred_element_type=F32)


def kernel(
    n, nrow, nl, kk, scale,
    x_ref, g_ref, psi_ref, far_ref, blk_ref, w_hbm, b_ref,
    out_hbm, gf_hbm, gw_ref, gb_ref,
    w_ref, out_ref, gf_ref, ecols, t_ref, loc_sem,
    hal, polf, polc, a_own, a_lr, a_t, a_j, a_farf, a_farc, zs, edge_acc,
    s0, r0, own, s1, r1, s2, r2, bsend, brecv,
    h_send, h_recv, p_send, p_recv, send0, recv0, send1, recv1, send2, recv2, b_ssem, b_rsem,
):
    part = lax.axis_index("parts")
    lat = lax.axis_index("lat")
    lon = lax.axis_index("lon")
    other = 1 - lat
    chan = x_ref.shape[1]
    half = chan // 2
    circle = n * nl
    nb = nrow // BR
    m = BR * nl * kk
    cells = BR * nl
    right = lax.rem(lon + 1, n)
    left = lax.rem(lon + n - 1, n)
    mine = lat * n + lon
    par = lax.rem(lon, 2)
    zz = lon // 2
    nz = n // 2
    rcp = pltpu.make_async_remote_copy
    load_w = pltpu.make_async_copy(w_hbm, w_ref, loc_sem.at[0])
    store_out = pltpu.make_async_copy(out_ref, out_hbm, loc_sem.at[1])
    store_gf = pltpu.make_async_copy(gf_ref, gf_hbm, loc_sem.at[2])
    load_w.start()

    barrier = pltpu.get_barrier_semaphore()

    def greet(step, _):
        to = lax.rem(mine + step, 2 * n)
        pl.semaphore_signal(
            barrier, inc=1, device_id=(part, to // n, lax.rem(to, n)), device_id_type=MESH
        )
        return 0

    lax.fori_loop(1, 2 * n, greet, 0)
    bsend[...] = jnp.broadcast_to(
        jnp.sum(g_ref[...].astype(F32), axis=0, keepdims=True), bsend.shape
    )
    rid = lax.broadcasted_iota(jnp.int32, (2 * nrow, nrow * nl), 0)
    cid = lax.broadcasted_iota(jnp.int32, (2 * nrow, nrow * nl), 1)
    want = lax.rem(rid, nrow) * nl + jnp.where(rid < nrow, 0, nl - 1)
    ends = (cid == want).astype(BF16)
    for d, src in enumerate((x_ref, g_ref)):
        picked = dot(ends, src[...]).astype(BF16)
        ecols[2 * d] = picked[:nrow]
        ecols[2 * d + 1] = picked[nrow:]
    pl.semaphore_wait(barrier, 2 * n - 1)

    srcs = (x_ref, g_ref)
    cut = pl.multiple_of(other * (nrow - 16), 16)
    cell_cut = pl.multiple_of(other * (nrow * nl - 16), 16)
    halo = []
    for d in range(2):
        first = ecols.at[2 * d]
        last = ecols.at[2 * d + 1]
        moves = (
            (last, 0, nrow, (part, lat, right)),
            (first, nrow, nrow, (part, lat, left)),
            (last.at[pl.ds(cut, 16)], 2 * nrow, 16, (part, other, right)),
            (first.at[pl.ds(cut, 16)], 2 * nrow + 16, 16, (part, other, left)),
            (srcs[d].at[pl.ds(cell_cut, 16)], 2 * nrow + 32, 16, (part, other, lon)),
        )
        for s, (src, start, size, to) in enumerate(moves):
            halo.append(
                rcp(
                    src_ref=src, dst_ref=hal.at[d, pl.ds(start, size)],
                    send_sem=h_send.at[d, s], recv_sem=h_recv.at[d, s],
                    device_id=to, device_id_type=MESH,
                )
            )

    def polar_copy(step, d):
        to = lax.rem(lon + step, n)
        buf, rows = ((polf, FROWS * nl), (polc, CROWS * nl))[d]
        return rcp(
            src_ref=srcs[d].at[pl.ds(0, rows)], dst_ref=buf.at[lon],
            send_sem=p_send.at[d, step], recv_sem=p_recv.at[d, step],
            device_id=(part, lat, to), device_id_type=MESH,
        )

    def bias_copy(step):
        to = lax.rem(mine + step, 2 * n)
        return rcp(
            src_ref=bsend, dst_ref=brecv.at[mine],
            send_sem=b_ssem.at[step], recv_sem=b_rsem.at[step],
            device_id=(part, to // n, lax.rem(to, n)), device_id_type=MESH,
        )

    def loop(lo, hi, body):
        def run(i, _):
            body(i)
            return 0

        lax.fori_loop(lo, hi, run, 0)

    for c in halo:
        c.start()

    @pl.when(lat == 0)
    def _():
        loop(1, n, lambda step: [polar_copy(step, d).start() for d in range(2)])
        polf[lon] = x_ref[0 : FROWS * nl, :]
        polc[lon] = g_ref[0 : CROWS * nl, :]

    loop(1, 2 * n, lambda step: bias_copy(step).start())
    brecv[mine] = bsend[...]

    nlat = psi_ref.shape[3]
    psi = jnp.concatenate(
        [psi_ref[w, e].astype(F32) for w in range(3) for e in range(3)], axis=0
    ).astype(BF16)

    def psi_rows(b):
        rid = lax.broadcasted_iota(jnp.int32, (3 * cells, nlat), 0)
        cid = lax.broadcasted_iota(jnp.int32, (3 * cells, nlat), 1)
        want = lat * nrow + b * BR + lax.rem(rid, cells) // nl + 1 - rid // cells
        return lax.dot_general(
            (cid == want).astype(BF16), psi, (((1,), (1,)), ((), ())),
            preferred_element_type=F32,
        )

    def taps(b, pv, rs, ls, qs, dst):
        width = rs.shape[1]
        rid = lax.broadcasted_iota(jnp.int32, (cells, width), 0)
        dr = rs - (rid // nl + b * BR) + 1
        dl = ls - lax.rem(rid, nl) + 1
        ok = (dr >= 0) & (dr < 3) & (dl >= 0) & (dl < 3)
        code = jnp.where(ok, dr * 3 + dl, -1)
        for d in range(2):
            for k in range(kk):
                vals = jnp.zeros((cells, width), F32)
                for q in qs:
                    w, at = (1, q * kk + k) if d == 0 else (2 - q // 3, (8 - q) * kk + k)
                    col = pv[w * cells : (w + 1) * cells, at : at + 1]
                    vals = jnp.where(code == q, col, vals)
                dst(d, k, vals.astype(BF16))

    def window(b):
        return jnp.clip(b * BR - 4, 0, nrow - 16)

    def build(b):
        pv = psi_rows(b)

        def put_own(d, k, vals):
            a_own[d, b, k * cells : (k + 1) * cells, :] = vals

        def put_lr(d, k, vals):
            a_lr[d, b, k * cells : (k + 1) * cells, :] = vals

        lane = lax.broadcasted_iota(jnp.int32, (cells, 16 * nl), 1)
        taps(b, pv, window(b) + lane // nl, lax.rem(lane, nl), range(9), put_own)
        lane = lax.broadcasted_iota(jnp.int32, (cells, 2 * nrow), 1)
        taps(
            b, pv, lax.rem(lane, nrow), jnp.where(lane < nrow, -1, nl), (0, 2, 3, 5, 6, 8), put_lr
        )

    loop(0, nb, build)
    lane = lax.broadcasted_iota(jnp.int32, (cells, 48), 1)
    rs = jnp.where(
        lane < 32,
        lax.rem(lane, 16) + jnp.where(lat == 0, nrow, -16),
        (lane - 32) // nl + jnp.where(lat == 0, nrow, -16 // nl),
    )
    ls = jnp.where(lane < 16, -1, jnp.where(lane < 32, nl, lax.rem(lane, nl)))

    def put_t(d, k, vals):
        a_t[d, k * cells : (k + 1) * cells, :] = vals

    eb = other * (nb - 1)
    taps(eb, psi_rows(eb), rs, ls, range(9), put_t)

    tr = kk * BR

    @pl.when(lat == 0)
    def _():
        rid = lax.broadcasted_iota(jnp.int32, (m, m), 0)
        cid = lax.broadcasted_iota(jnp.int32, (m, m), 1)
        frows, bw = far_ref.shape
        ns, npol = blk_ref.shape
        lane = lax.broadcasted_iota(jnp.int32, (bw, circle), 1)
        spread = (lax.broadcasted_iota(jnp.int32, (bw, circle), 0) == lax.rem(lane, bw)).astype(BF16)
        frow = lax.broadcasted_iota(jnp.int32, (frows, circle), 0) // (3 * kk)
        block = jnp.zeros((frows, circle), jnp.int32)
        for q in range(npol * ns):
            block = jnp.where(frow == q, blk_ref[q % ns, q // ns], block)
        lane = lax.broadcasted_iota(jnp.int32, (frows, circle), 1)
        named = jnp.where(block == lane // bw, dot(far_ref[...], spread), 0.0).astype(BF16)
        trow = lax.broadcasted_iota(jnp.int32, (6 * tr, frows), 0)
        srow = lax.broadcasted_iota(jnp.int32, (6 * tr, frows), 1)
        t_i = lax.rem(trow, BR)
        t_wk = lax.rem(trow, 3 * tr) // BR
        t_p = jnp.where(trow < 3 * tr, t_i, t_i - t_wk // kk + 1)
        pick_row = (lax.rem(srow, 3 * kk) == t_wk) & (srow // (3 * kk * ns) == t_p)
        t_ref[...] = dot(pick_row.astype(BF16), named).astype(BF16)
        order = ((rid // nl == lax.rem(cid, tr)) & (lax.rem(rid, nl) == cid // tr)).astype(BF16)
        for d, rows in ((0, FROWS), (1, CROWS)):
            wide = GROUP * rows * nl

            def far_group(grp, d=d, rows=rows, wide=wide):
                lane = lax.broadcasted_iota(jnp.int32, (circle, wide), 1)
                t_id = lax.broadcasted_iota(jnp.int32, (circle, wide), 0)
                lon_of = (grp * GROUP + lane // (rows * nl)) * nl + lax.rem(lane, nl)
                rlane = lax.broadcasted_iota(jnp.int32, (tr, wide), 1)
                r_of = lax.rem(rlane // nl, rows)
                i_of = lax.rem(lax.broadcasted_iota(jnp.int32, (tr, wide), 0), BR)
                dist = lon_of - lon * nl + circle
                for j in range(nl):
                    if d == 0:
                        t_want = lax.rem(dist - j + circle, circle)
                    else:
                        t_want = lax.rem(2 * circle - dist + j + circle, circle)
                    pick = (t_id == t_want).astype(BF16)
                    full = dot(t_ref[d * 3 * tr : (d + 1) * 3 * tr, :], pick)
                    acc = jnp.zeros((tr, wide), F32)
                    for w in range(3):
                        hit = (r_of - i_of + 1 == w) if d == 0 else (i_of - r_of + 1 == w)
                        acc = jnp.where(hit, full[w * tr : (w + 1) * tr], acc)
                    a_j[j * tr : (j + 1) * tr, 0:wide] = acc.astype(BF16)
                dst = a_farf if d == 0 else a_farc
                dst[grp] = dot(order, a_j[:, 0:wide]).astype(BF16)

            loop(0, n // GROUP, far_group)

    def near(d, b):
        start = window(b) * nl
        start = pl.multiple_of(start, 16)
        return dot(a_own[d, b], srcs[d][pl.ds(start, 16 * nl), :]) + dot(
            a_lr[d, b], hal[d, 0 : 2 * nrow, :]
        )

    def put(d, b, acc):
        at = pl.multiple_of(b * cells, cells)
        for k in range(kk):
            zs[d, k, pl.ds(at, cells), :] = acc[k * cells : (k + 1) * cells].astype(BF16)

    def inner(d):
        loop(1, nb - 1, lambda b: put(d, b, near(d, b)))

    def edges(d):
        edge_acc[0] = near(d, jnp.int32(0))
        edge_acc[1] = near(d, jnp.int32(nb - 1))
        edge_acc[other] += dot(a_t[d], hal[d, 2 * nrow : 2 * nrow + 48, :])

        @pl.when(lat == 0)
        def _():
            loop(1, n, lambda step: polar_copy(step, d).wait())
            buf, coefs, rows = ((polf, a_farf, FROWS), (polc, a_farc, CROWS))[d]

            def far_add(grp):
                src = buf[pl.ds(grp * GROUP, GROUP)].reshape(GROUP * rows * nl, chan)
                edge_acc[0] += dot(coefs[grp], src)

            loop(0, n // GROUP, far_add)

        put(d, jnp.int32(0), edge_acc[0])
        put(d, jnp.int32(nb - 1), edge_acc[1])

    for c in halo:
        c.wait()
    inner(0)
    edges(0)

    def copy0(k):
        return rcp(
            src_ref=s0.at[k], dst_ref=r0.at[k], send_sem=send0.at[k], recv_sem=recv0.at[k],
            device_id=(part, other, lon), device_id_type=MESH,
        )

    def copy1(k):
        return rcp(
            src_ref=s1.at[k], dst_ref=r1.at[k], send_sem=send1.at[k], recv_sem=recv1.at[k],
            device_id=(part, lat, lon + 1 - 2 * par), device_id_type=MESH,
        )

    def copy2(k, step):
        to = lax.rem(zz + step, nz)
        return rcp(
            src_ref=s2.at[k, to], dst_ref=r2.at[k, zz],
            send_sem=send2.at[k, step], recv_sem=recv2.at[k, step],
            device_id=(part, lat, to * 2 + par), device_id_type=MESH,
        )

    def grads(k, which):
        z = zs[0, k, :, pl.ds(pl.multiple_of(which * half, half), half)]
        return lax.dot_general(
            z, g_ref[...], (((0,), (0,)), ((), ())), preferred_element_type=F32
        )

    def stage0(k):
        s0[k] = grads(k, other).astype(BF16)
        copy0(k).start()

    def keep(k):
        own[k] = grads(k, lat).reshape(own.shape[1:])

    loop(0, kk, stage0)
    loop(0, kk, keep)

    def stage1(k):
        copy0(k).wait()
        own[k] += r0[k].astype(F32).reshape(own.shape[1:])
        for q in range(nz):
            s1[k, q] = own[k, q, 1 - par].astype(BF16)
        copy1(k).start()

    loop(0, kk, stage1)

    step_rows = 256

    def forward(b):
        at = pl.ds(pl.multiple_of(b * step_rows, step_rows), step_rows)
        acc = dot(zs[0, 0, at, :], w_ref[0])
        for k in range(1, kk):
            acc += dot(zs[0, k, at, :], w_ref[k])
        out_ref[at, :] = (acc + b_ref[...]).astype(BF16)

    load_w.wait()
    loop(0, nrow * nl // step_rows, forward)
    store_out.start()

    def stage2(k):
        copy1(k).wait()
        for q in range(nz):
            own[k, q, par] += r1[k, q].astype(F32)
            s2[k, q] = own[k, q, par].astype(BF16)
        loop(1, nz, lambda step: copy2(k, step).start())

    loop(0, kk, stage2)

    inner(1)
    edges(1)

    def backward(b):
        at = pl.ds(pl.multiple_of(b * step_rows, step_rows), step_rows)
        acc = None
        for k in range(kk):
            term = lax.dot_general(
                zs[1, k, at, :], w_ref[k], (((1,), (1,)), ((), ())), preferred_element_type=F32
            )
            acc = term if acc is None else acc + term
        gf_ref[at, :] = acc.astype(BF16)

    loop(0, nrow * nl // step_rows, backward)
    store_gf.start()

    loop(1, 2 * n, lambda step: bias_copy(step).wait())
    gb_ref[...] = jnp.sum(brecv[...], axis=0) * scale

    def final(k):
        gw_ref[k] = own[k, zz, par]

        def take(step):
            copy2(k, step).wait()
            gw_ref[k] += r2[k, lax.rem(zz + nz - step, nz)].astype(F32)

        loop(1, nz, take)
        gw_ref[k] = gw_ref[k] * scale

    loop(0, kk, final)
    store_out.wait()
    store_gf.wait()


def hand_on(n, out_in, gf_in, gw_in, gb_in, out_ref, gf_ref, gw_ref, gb_ref, sem):
    copies = []
    for a, (src, dst) in enumerate(((out_in, out_ref), (gf_in, gf_ref), (gw_in, gw_ref))):
        count = sem.shape[1]
        size = src.shape[0] // count
        for c in range(count):
            at = pl.ds(c * size, size)
            copies.append(pltpu.make_async_copy(src.at[at], dst.at[at], sem.at[a, c]))
    for c in copies:
        c.start()
    share = gb_ref.shape[1]
    chan = gb_in.shape[1]
    place = lax.axis_index("lat") * n + lax.axis_index("lon")
    gb_ref[...] = pltpu.roll(gb_in[...], lax.rem(chan - place * share, chan), 1)[0:1, :share]
    for c in copies:
        c.wait()


def on_device(fields, psi_near, psi_far, blocks, weight, out_bias, cotangent):
    nrow, nl, chan = fields.shape
    kk = weight.shape[0]
    npol, ns, _, _, bw = psi_far.shape
    n = lax.axis_size("lon")
    circle = n * nl
    nb = nrow // BR
    m = BR * nl * kk
    taps = psi_near.transpose(2, 3, 1, 0)
    far = psi_far.transpose(0, 1, 3, 2, 4).reshape(npol * ns * 3 * kk, bw)
    lat_count = lax.axis_size("lat")
    scale = 1.0 / math.sqrt(nrow * lat_count * circle)
    nz = n // 2
    cr = chan // 2 // n
    vmem = pl.BlockSpec(memory_space=pltpu.VMEM)
    anywhere = pl.BlockSpec(memory_space=pl.ANY)
    dma = pltpu.SemaphoreType.DMA
    ng = n // GROUP
    out, gf, gw, gb = pl.pallas_call(
        functools.partial(kernel, n, nrow, nl, kk, scale),
        out_shape=(
            jax.ShapeDtypeStruct((nrow * nl, chan), BF16),
            jax.ShapeDtypeStruct((nrow * nl, chan), BF16),
            jax.ShapeDtypeStruct((kk, cr, chan), F32),
            jax.ShapeDtypeStruct((8, chan), F32),
        ),
        in_specs=[vmem] * 4 + [pl.BlockSpec(memory_space=pltpu.SMEM), anywhere, vmem],
        out_specs=(anywhere, anywhere, vmem, vmem),
        scratch_shapes=[
            pltpu.VMEM(weight.shape, BF16),
            pltpu.VMEM((nrow * nl, chan), BF16),
            pltpu.VMEM((nrow * nl, chan), BF16),
            pltpu.VMEM((4, nrow, chan), BF16),
            pltpu.VMEM((6 * kk * BR, circle), BF16),
            dma((3,)),
            pltpu.VMEM((2, 2 * nrow + 48, chan), BF16),
            pltpu.VMEM((n, FROWS * nl, chan), BF16),
            pltpu.VMEM((n, CROWS * nl, chan), BF16),
            pltpu.VMEM((2, nb, m, 16 * nl), BF16),
            pltpu.VMEM((2, nb, m, 2 * nrow), BF16),
            pltpu.VMEM((2, m, 48), BF16),
            pltpu.VMEM((m, GROUP * FROWS * nl), BF16),
            pltpu.VMEM((ng, m, GROUP * FROWS * nl), BF16),
            pltpu.VMEM((ng, m, GROUP * CROWS * nl), BF16),
            pltpu.VMEM((2, kk, nrow * nl, chan), BF16),
            pltpu.VMEM((2, m, chan), F32),
            pltpu.VMEM((kk, chan // 2, chan), BF16),
            pltpu.VMEM((kk, chan // 2, chan), BF16),
            pltpu.VMEM((kk, nz, 2, cr, chan), F32),
            pltpu.VMEM((kk, nz, cr, chan), BF16),
            pltpu.VMEM((kk, nz, cr, chan), BF16),
            pltpu.VMEM((kk, nz, cr, chan), BF16),
            pltpu.VMEM((kk, nz, cr, chan), BF16),
            pltpu.VMEM((8, chan), F32),
            pltpu.VMEM((2 * n, 8, chan), F32),
            dma((2, 5)), dma((2, 5)),
            dma((2, n)), dma((2, n)),
            dma((kk,)), dma((kk,)),
            dma((kk,)), dma((kk,)),
            dma((kk, nz)), dma((kk, nz)),
            dma((2 * n,)), dma((2 * n,)),
        ],
        compiler_params=pltpu.CompilerParams(
            collective_id=0, has_side_effects=True, vmem_limit_bytes=56 * 1024 * 1024
        ),
        cost_estimate=pl.CostEstimate(
            flops=8 * nrow * nl * kk * chan * chan, bytes_accessed=8 << 20, transcendentals=0
        ),
    )(
        fields.reshape(nrow * nl, chan),
        cotangent.reshape(nrow * nl, chan),
        taps, far, blocks.T, weight, out_bias.reshape(1, chan),
    )
    share = chan // (lat_count * n)
    out, gf, gw, gb = pl.pallas_call(
        functools.partial(hand_on, n),
        out_shape=(
            jax.ShapeDtypeStruct(out.shape, BF16),
            jax.ShapeDtypeStruct(gf.shape, BF16),
            jax.ShapeDtypeStruct(gw.shape, F32),
            jax.ShapeDtypeStruct((1, share), F32),
        ),
        in_specs=[vmem] * 4,
        out_specs=(anywhere,) * 3 + (vmem,),
        scratch_shapes=[dma((3, kk))],
    )(out, gf, gw, gb)
    return (out.reshape(fields.shape), gf.reshape(fields.shape), gw, gb.reshape(share))


def solution(mesh):
    return jax.shard_map(
        on_device,
        mesh=mesh,
        in_specs=(
            P(("parts", "lat"), "lon", None), P(), P(), P(), P(), P(),
            P(("parts", "lat"), "lon", None),
        ),
        out_specs=(
            P(("parts", "lat"), "lon", None),
            P(("parts", "lat"), "lon", None),
            P(None, ("parts", "lat", "lon"), None),
            P(("parts", "lat", "lon")),
        ),
        check_vma=False,
    )
```

```python
import functools
import math

import jax
import jax.numpy as jnp
from jax import lax
from jax.experimental import pallas as pl
from jax.experimental.pallas import tpu as pltpu
from jax.sharding import PartitionSpec as P

F32 = jnp.float32
BF16 = jnp.bfloat16
MESH = pl.DeviceIdType.MESH
BR = 8
FROWS = 6
CROWS = 4
GROUP = 8


def dot(a, b):
    return jnp.dot(a, b, preferred_element_type=F32)


def kernel(
    n, nrow, nl, kk, scale,
    x_ref, g_ref, psi_ref, far_ref, blk_ref, w_hbm, b_ref,
    out_hbm, gf_hbm, gw_ref, gb_ref,
    w_ref, out_ref, gf_ref, ecols, t_ref, loc_sem,
    hal, polf, polc, a_own, a_lr, a_t, a_j, a_farf, a_farc, zs, edge_acc,
    s0, r0, own, s1, r1, s2, r2, bsend, brecv,
    h_send, h_recv, p_send, p_recv, send0, recv0, send1, recv1, send2, recv2, b_ssem, b_rsem,
):
    part = lax.axis_index("parts")
    lat = lax.axis_index("lat")
    lon = lax.axis_index("lon")
    other = 1 - lat
    chan = x_ref.shape[1]
    half = chan // 2
    circle = n * nl
    nb = nrow // BR
    m = BR * nl * kk
    cells = BR * nl
    right = lax.rem(lon + 1, n)
    left = lax.rem(lon + n - 1, n)
    mine = lat * n + lon
    par = lax.rem(lon, 2)
    zz = lon // 2
    nz = n // 2
    rcp = pltpu.make_async_remote_copy
    load_w = pltpu.make_async_copy(w_hbm, w_ref, loc_sem.at[0])
    store_out = pltpu.make_async_copy(out_ref, out_hbm, loc_sem.at[1])
    store_gf = pltpu.make_async_copy(gf_ref, gf_hbm, loc_sem.at[2])
    load_w.start()

    barrier = pltpu.get_barrier_semaphore()

    def greet(step, _):
        to = lax.rem(mine + step, 2 * n)
        pl.semaphore_signal(
            barrier, inc=1, device_id=(part, to // n, lax.rem(to, n)), device_id_type=MESH
        )
        return 0

    lax.fori_loop(1, 2 * n, greet, 0)
    bsend[...] = jnp.sum(g_ref[...].astype(F32), axis=0, keepdims=True)
    rid = lax.broadcasted_iota(jnp.int32, (2 * nrow, nrow * nl), 0)
    cid = lax.broadcasted_iota(jnp.int32, (2 * nrow, nrow * nl), 1)
    want = lax.rem(rid, nrow) * nl + jnp.where(rid < nrow, 0, nl - 1)
    ends = (cid == want).astype(BF16)
    for d, src in enumerate((x_ref, g_ref)):
        picked = dot(ends, src[...]).astype(BF16)
        ecols[2 * d] = picked[:nrow]
        ecols[2 * d + 1] = picked[nrow:]
    pl.semaphore_wait(barrier, 2 * n - 1)

    srcs = (x_ref, g_ref)
    cut = pl.multiple_of(other * (nrow - 16), 16)
    cell_cut = pl.multiple_of(other * (nrow * nl - 16), 16)
    halo = []
    for d in range(2):
        first = ecols.at[2 * d]
        last = ecols.at[2 * d + 1]
        moves = (
            (last, 0, nrow, (part, lat, right)),
            (first, nrow, nrow, (part, lat, left)),
            (last.at[pl.ds(cut, 16)], 2 * nrow, 16, (part, other, right)),
            (first.at[pl.ds(cut, 16)], 2 * nrow + 16, 16, (part, other, left)),
            (srcs[d].at[pl.ds(cell_cut, 16)], 2 * nrow + 32, 16, (part, other, lon)),
        )
        for s, (src, start, size, to) in enumerate(moves):
            halo.append(
                rcp(
                    src_ref=src, dst_ref=hal.at[d, pl.ds(start, size)],
                    send_sem=h_send.at[d, s], recv_sem=h_recv.at[d, s],
                    device_id=to, device_id_type=MESH,
                )
            )

    def polar_copy(step, d):
        to = lax.rem(lon + step, n)
        buf, rows = ((polf, FROWS * nl), (polc, CROWS * nl))[d]
        return rcp(
            src_ref=srcs[d].at[pl.ds(0, rows)], dst_ref=buf.at[lon],
            send_sem=p_send.at[d, step], recv_sem=p_recv.at[d, step],
            device_id=(part, lat, to), device_id_type=MESH,
        )

    def bias_copy(step):
        to = lax.rem(mine + step, 2 * n)
        return rcp(
            src_ref=bsend, dst_ref=brecv.at[mine],
            send_sem=b_ssem.at[step], recv_sem=b_rsem.at[step],
            device_id=(part, to // n, lax.rem(to, n)), device_id_type=MESH,
        )

    def loop(lo, hi, body):
        def run(i, _):
            body(i)
            return 0

        lax.fori_loop(lo, hi, run, 0)

    for c in halo:
        c.start()

    @pl.when(lat == 0)
    def _():
        loop(1, n, lambda step: [polar_copy(step, d).start() for d in range(2)])
        polf[lon] = x_ref[0 : FROWS * nl, :]
        polc[lon] = g_ref[0 : CROWS * nl, :]

    loop(1, 2 * n, lambda step: bias_copy(step).start())
    brecv[mine] = bsend[...]

    nlat = psi_ref.shape[3]
    psi = jnp.concatenate(
        [psi_ref[w, e].astype(F32) for w in range(3) for e in range(3)], axis=0
    ).astype(BF16)

    def psi_rows(b):
        rid = lax.broadcasted_iota(jnp.int32, (3 * cells, nlat), 0)
        cid = lax.broadcasted_iota(jnp.int32, (3 * cells, nlat), 1)
        want = lat * nrow + b * BR + lax.rem(rid, cells) // nl + 1 - rid // cells
        return lax.dot_general(
            (cid == want).astype(BF16), psi, (((1,), (1,)), ((), ())),
            preferred_element_type=F32,
        )

    def taps(b, pv, rs, ls, qs, dst):
        width = rs.shape[1]
        rid = lax.broadcasted_iota(jnp.int32, (cells, width), 0)
        dr = rs - (rid // nl + b * BR) + 1
        dl = ls - lax.rem(rid, nl) + 1
        ok = (dr >= 0) & (dr < 3) & (dl >= 0) & (dl < 3)
        code = jnp.where(ok, dr * 3 + dl, -1)
        for d in range(2):
            for k in range(kk):
                vals = jnp.zeros((cells, width), F32)
                for q in qs:
                    w, at = (1, q * kk + k) if d == 0 else (2 - q // 3, (8 - q) * kk + k)
                    col = pv[w * cells : (w + 1) * cells, at : at + 1]
                    vals = jnp.where(code == q, col, vals)
                dst(d, k, vals.astype(BF16))

    def window(b):
        return jnp.clip(b * BR - 4, 0, nrow - 16)

    def build(b):
        pv = psi_rows(b)

        def put_own(d, k, vals):
            a_own[d, b, k * cells : (k + 1) * cells, :] = vals

        def put_lr(d, k, vals):
            a_lr[d, b, k * cells : (k + 1) * cells, :] = vals

        lane = lax.broadcasted_iota(jnp.int32, (cells, 16 * nl), 1)
        taps(b, pv, window(b) + lane // nl, lax.rem(lane, nl), range(9), put_own)
        lane = lax.broadcasted_iota(jnp.int32, (cells, 2 * nrow), 1)
        taps(
            b, pv, lax.rem(lane, nrow), jnp.where(lane < nrow, -1, nl), (0, 2, 3, 5, 6, 8), put_lr
        )

    loop(0, nb, build)
    lane = lax.broadcasted_iota(jnp.int32, (cells, 48), 1)
    rs = jnp.where(
        lane < 32,
        lax.rem(lane, 16) + jnp.where(lat == 0, nrow, -16),
        (lane - 32) // nl + jnp.where(lat == 0, nrow, -16 // nl),
    )
    ls = jnp.where(lane < 16, -1, jnp.where(lane < 32, nl, lax.rem(lane, nl)))

    def put_t(d, k, vals):
        a_t[d, k * cells : (k + 1) * cells, :] = vals

    eb = other * (nb - 1)
    taps(eb, psi_rows(eb), rs, ls, range(9), put_t)

    tr = kk * BR

    @pl.when(lat == 0)
    def _():
        rid = lax.broadcasted_iota(jnp.int32, (m, m), 0)
        cid = lax.broadcasted_iota(jnp.int32, (m, m), 1)
        frows, bw = far_ref.shape
        ns, npol = blk_ref.shape
        lane = lax.broadcasted_iota(jnp.int32, (bw, circle), 1)
        spread = (lax.broadcasted_iota(jnp.int32, (bw, circle), 0) == lax.rem(lane, bw)).astype(BF16)
        frow = lax.broadcasted_iota(jnp.int32, (frows, circle), 0) // (3 * kk)
        block = jnp.zeros((frows, circle), jnp.int32)
        for q in range(npol * ns):
            block = jnp.where(frow == q, blk_ref[q % ns, q // ns], block)
        lane = lax.broadcasted_iota(jnp.int32, (frows, circle), 1)
        named = jnp.where(block == lane // bw, dot(far_ref[...], spread), 0.0).astype(BF16)
        trow = lax.broadcasted_iota(jnp.int32, (6 * tr, frows), 0)
        srow = lax.broadcasted_iota(jnp.int32, (6 * tr, frows), 1)
        t_i = lax.rem(trow, BR)
        t_wk = lax.rem(trow, 3 * tr) // BR
        t_p = jnp.where(trow < 3 * tr, t_i, t_i - t_wk // kk + 1)
        pick_row = (lax.rem(srow, 3 * kk) == t_wk) & (srow // (3 * kk * ns) == t_p)
        t_ref[...] = dot(pick_row.astype(BF16), named).astype(BF16)
        order = ((rid // nl == lax.rem(cid, tr)) & (lax.rem(rid, nl) == cid // tr)).astype(BF16)
        for d, rows in ((0, FROWS), (1, CROWS)):
            wide = GROUP * rows * nl

            def far_group(grp, d=d, rows=rows, wide=wide):
                lane = lax.broadcasted_iota(jnp.int32, (circle, wide), 1)
                t_id = lax.broadcasted_iota(jnp.int32, (circle, wide), 0)
                lon_of = (grp * GROUP + lane // (rows * nl)) * nl + lax.rem(lane, nl)
                rlane = lax.broadcasted_iota(jnp.int32, (tr, wide), 1)
                r_of = lax.rem(rlane // nl, rows)
                i_of = lax.rem(lax.broadcasted_iota(jnp.int32, (tr, wide), 0), BR)
                dist = lon_of - lon * nl + circle
                for j in range(nl):
                    if d == 0:
                        t_want = lax.rem(dist - j + circle, circle)
                    else:
                        t_want = lax.rem(2 * circle - dist + j + circle, circle)
                    pick = (t_id == t_want).astype(BF16)
                    full = dot(t_ref[d * 3 * tr : (d + 1) * 3 * tr, :], pick)
                    acc = jnp.zeros((tr, wide), F32)
                    for w in range(3):
                        hit = (r_of - i_of + 1 == w) if d == 0 else (i_of - r_of + 1 == w)
                        acc = jnp.where(hit, full[w * tr : (w + 1) * tr], acc)
                    a_j[j * tr : (j + 1) * tr, 0:wide] = acc.astype(BF16)
                dst = a_farf if d == 0 else a_farc
                dst[grp] = dot(order, a_j[:, 0:wide]).astype(BF16)

            loop(0, n // GROUP, far_group)

    def near(d, b):
        start = window(b) * nl
        start = pl.multiple_of(start, 16)
        return dot(a_own[d, b], srcs[d][pl.ds(start, 16 * nl), :]) + dot(
            a_lr[d, b], hal[d, 0 : 2 * nrow, :]
        )

    def put(d, b, acc):
        at = pl.multiple_of(b * cells, cells)
        for k in range(kk):
            zs[d, k, pl.ds(at, cells), :] = acc[k * cells : (k + 1) * cells].astype(BF16)

    def inner(d):
        loop(1, nb - 1, lambda b: put(d, b, near(d, b)))

    def edges(d):
        edge_acc[0] = near(d, jnp.int32(0))
        edge_acc[1] = near(d, jnp.int32(nb - 1))
        edge_acc[other] += dot(a_t[d], hal[d, 2 * nrow : 2 * nrow + 48, :])

        @pl.when(lat == 0)
        def _():
            loop(1, n, lambda step: polar_copy(step, d).wait())
            buf, coefs, rows = ((polf, a_farf, FROWS), (polc, a_farc, CROWS))[d]

            def far_add(grp):
                src = buf[pl.ds(grp * GROUP, GROUP)].reshape(GROUP * rows * nl, chan)
                edge_acc[0] += dot(coefs[grp], src)

            loop(0, n // GROUP, far_add)

        put(d, jnp.int32(0), edge_acc[0])
        put(d, jnp.int32(nb - 1), edge_acc[1])

    for c in halo:
        c.wait()
    inner(0)
    edges(0)

    def copy0(k):
        return rcp(
            src_ref=s0.at[k], dst_ref=r0.at[k], send_sem=send0.at[k], recv_sem=recv0.at[k],
            device_id=(part, other, lon), device_id_type=MESH,
        )

    def copy1(k):
        return rcp(
            src_ref=s1.at[k], dst_ref=r1.at[k], send_sem=send1.at[k], recv_sem=recv1.at[k],
            device_id=(part, lat, lon + 1 - 2 * par), device_id_type=MESH,
        )

    def copy2(k, step):
        to = lax.rem(zz + step, nz)
        return rcp(
            src_ref=s2.at[k, to], dst_ref=r2.at[k, zz],
            send_sem=send2.at[k, step], recv_sem=recv2.at[k, step],
            device_id=(part, lat, to * 2 + par), device_id_type=MESH,
        )

    def grads(k, which):
        z = zs[0, k, :, pl.ds(pl.multiple_of(which * half, half), half)]
        return lax.dot_general(
            z, g_ref[...], (((0,), (0,)), ((), ())), preferred_element_type=F32
        )

    def stage0(k):
        s0[k] = grads(k, other).astype(BF16)
        copy0(k).start()

    def keep(k):
        own[k] = grads(k, lat).reshape(own.shape[1:])

    loop(0, kk, stage0)
    loop(0, kk, keep)

    def stage1(k):
        copy0(k).wait()
        own[k] += r0[k].astype(F32).reshape(own.shape[1:])
        for q in range(nz):
            s1[k, q] = own[k, q, 1 - par].astype(BF16)
        copy1(k).start()

    loop(0, kk, stage1)

    step_rows = 256

    def forward(b):
        at = pl.ds(pl.multiple_of(b * step_rows, step_rows), step_rows)
        acc = dot(zs[0, 0, at, :], w_ref[0])
        for k in range(1, kk):
            acc += dot(zs[0, k, at, :], w_ref[k])
        out_ref[at, :] = (acc + b_ref[...]).astype(BF16)

    load_w.wait()
    loop(0, nrow * nl // step_rows, forward)
    store_out.start()

    def stage2(k):
        copy1(k).wait()
        for q in range(nz):
            own[k, q, par] += r1[k, q].astype(F32)
            s2[k, q] = own[k, q, par].astype(BF16)
        loop(1, nz, lambda step: copy2(k, step).start())


    def backward(b):
        at = pl.ds(pl.multiple_of(b * step_rows, step_rows), step_rows)
        acc = None
        for k in range(kk):
            term = lax.dot_general(
                zs[1, k, at, :], w_ref[k], (((1,), (1,)), ((), ())), preferred_element_type=F32
            )
            acc = term if acc is None else acc + term
        gf_ref[at, :] = acc.astype(BF16)

    stage2(0)
    inner(1)
    stage2(1)
    edges(1)
    loop(2, kk - 1, stage2)
    loop(0, nrow * nl // step_rows, backward)
    store_gf.start()
    stage2(kk - 1)

    loop(1, 2 * n, lambda step: bias_copy(step).wait())
    gb_ref[...] = jnp.broadcast_to(jnp.sum(brecv[...], axis=0) * scale, gb_ref.shape)

    def final(k):
        gw_ref[k] = own[k, zz, par]

        def take(step):
            copy2(k, step).wait()
            gw_ref[k] += r2[k, lax.rem(zz + nz - step, nz)].astype(F32)

        loop(1, nz, take)
        gw_ref[k] = gw_ref[k] * scale

    loop(0, kk, final)
    store_out.wait()
    store_gf.wait()


def hand_on(n, out_in, gf_in, gw_in, gb_in, out_ref, gf_ref, gw_ref, gb_ref, sem):
    copies = []
    for a, (src, dst) in enumerate(((out_in, out_ref), (gf_in, gf_ref), (gw_in, gw_ref))):
        count = sem.shape[1]
        size = src.shape[0] // count
        for c in range(count):
            at = pl.ds(c * size, size)
            copies.append(pltpu.make_async_copy(src.at[at], dst.at[at], sem.at[a, c]))
    for c in copies:
        c.start()
    share = gb_ref.shape[1]
    chan = gb_in.shape[1]
    place = lax.axis_index("lat") * n + lax.axis_index("lon")
    gb_ref[...] = pltpu.roll(gb_in[...], lax.rem(chan - place * share, chan), 1)[0:1, :share]
    for c in copies:
        c.wait()


def on_device(fields, psi_near, psi_far, blocks, weight, out_bias, cotangent):
    nrow, nl, chan = fields.shape
    kk = weight.shape[0]
    npol, ns, _, _, bw = psi_far.shape
    n = lax.axis_size("lon")
    circle = n * nl
    nb = nrow // BR
    m = BR * nl * kk
    taps = psi_near.transpose(2, 3, 1, 0)
    far = psi_far.transpose(0, 1, 3, 2, 4).reshape(npol * ns * 3 * kk, bw)
    lat_count = lax.axis_size("lat")
    scale = 1.0 / math.sqrt(nrow * lat_count * circle)
    nz = n // 2
    cr = chan // 2 // n
    vmem = pl.BlockSpec(memory_space=pltpu.VMEM)
    anywhere = pl.BlockSpec(memory_space=pl.ANY)
    dma = pltpu.SemaphoreType.DMA
    ng = n // GROUP
    out, gf, gw, gb = pl.pallas_call(
        functools.partial(kernel, n, nrow, nl, kk, scale),
        out_shape=(
            jax.ShapeDtypeStruct((nrow * nl, chan), BF16),
            jax.ShapeDtypeStruct((nrow * nl, chan), BF16),
            jax.ShapeDtypeStruct((kk, cr, chan), F32),
            jax.ShapeDtypeStruct((8, chan), F32),
        ),
        in_specs=[vmem] * 4 + [pl.BlockSpec(memory_space=pltpu.SMEM), anywhere, vmem],
        out_specs=(anywhere, anywhere, vmem, vmem),
        scratch_shapes=[
            pltpu.VMEM(weight.shape, BF16),
            pltpu.VMEM((nrow * nl, chan), BF16),
            pltpu.VMEM((nrow * nl, chan), BF16),
            pltpu.VMEM((4, nrow, chan), BF16),
            pltpu.VMEM((6 * kk * BR, circle), BF16),
            dma((3,)),
            pltpu.VMEM((2, 2 * nrow + 48, chan), BF16),
            pltpu.VMEM((n, FROWS * nl, chan), BF16),
            pltpu.VMEM((n, CROWS * nl, chan), BF16),
            pltpu.VMEM((2, nb, m, 16 * nl), BF16),
            pltpu.VMEM((2, nb, m, 2 * nrow), BF16),
            pltpu.VMEM((2, m, 48), BF16),
            pltpu.VMEM((m, GROUP * FROWS * nl), BF16),
            pltpu.VMEM((ng, m, GROUP * FROWS * nl), BF16),
            pltpu.VMEM((ng, m, GROUP * CROWS * nl), BF16),
            pltpu.VMEM((2, kk, nrow * nl, chan), BF16),
            pltpu.VMEM((2, m, chan), F32),
            pltpu.VMEM((kk, chan // 2, chan), BF16),
            pltpu.VMEM((kk, chan // 2, chan), BF16),
            pltpu.VMEM((kk, nz, 2, cr, chan), F32),
            pltpu.VMEM((kk, nz, cr, chan), BF16),
            pltpu.VMEM((kk, nz, cr, chan), BF16),
            pltpu.VMEM((kk, nz, cr, chan), BF16),
            pltpu.VMEM((kk, nz, cr, chan), BF16),
            pltpu.VMEM((1, chan), F32),
            pltpu.VMEM((2 * n, 1, chan), F32),
            dma((2, 5)), dma((2, 5)),
            dma((2, n)), dma((2, n)),
            dma((kk,)), dma((kk,)),
            dma((kk,)), dma((kk,)),
            dma((kk, nz)), dma((kk, nz)),
            dma((2 * n,)), dma((2 * n,)),
        ],
        compiler_params=pltpu.CompilerParams(
            collective_id=0, has_side_effects=True, vmem_limit_bytes=56 * 1024 * 1024
        ),
        cost_estimate=pl.CostEstimate(
            flops=8 * nrow * nl * kk * chan * chan, bytes_accessed=8 << 20, transcendentals=0
        ),
    )(
        fields.reshape(nrow * nl, chan),
        cotangent.reshape(nrow * nl, chan),
        taps, far, blocks.T, weight, out_bias.reshape(1, chan),
    )
    share = chan // (lat_count * n)
    out, gf, gw, gb = pl.pallas_call(
        functools.partial(hand_on, n),
        out_shape=(
            jax.ShapeDtypeStruct(out.shape, BF16),
            jax.ShapeDtypeStruct(gf.shape, BF16),
            jax.ShapeDtypeStruct(gw.shape, F32),
            jax.ShapeDtypeStruct((1, share), F32),
        ),
        in_specs=[vmem] * 4,
        out_specs=(anywhere,) * 3 + (vmem,),
        scratch_shapes=[dma((3, kk))],
    )(out, gf, gw, gb)
    return (out.reshape(fields.shape), gf.reshape(fields.shape), gw, gb.reshape(share))


def solution(mesh):
    return jax.shard_map(
        on_device,
        mesh=mesh,
        in_specs=(
            P(("parts", "lat"), "lon", None), P(), P(), P(), P(), P(),
            P(("parts", "lat"), "lon", None),
        ),
        out_specs=(
            P(("parts", "lat"), "lon", None),
            P(("parts", "lat"), "lon", None),
            P(None, ("parts", "lat", "lon"), None),
            P(("parts", "lat", "lon")),
        ),
        check_vma=False,
    )
```
